128 devices in a mesh: seq: 8 (over z, core), head: 16 (over y, x).
Axes of the slice: x: 4, y: 4, z: 4, core: 2. Of those that a mesh axis runs over, the one named last changes fastest.
Arguments:
- queries: bfloat16 [32768, 4096], P(('seq', 'head')), may hold values from -8 to 8
- keys: bfloat16 [32768, 4096], P(('seq', 'head')), may hold values from -8 to 8
- values: bfloat16 [32768, 4096], P(('seq', 'head')), may hold values from -6 to 6
- head_kind: int32 [32], replicated, may hold values 0 or 1
Outputs:
- attended: bfloat16 [32768, 4096], P(('seq', 'head'))
The draws below stay inside these ranges and needn't reach their ends.
All inputs are finite; a program needn't handle non-finite values.
Results may differ from the reference program's by a relative error of at most 0.012.
Values may be sent and summed in bfloat16 or wider, within the bound.
No kernel may reach another device: no remote copies, remote signals or barrier semaphores. Data moves between devices by JAX's collectives and lax.ppermute only.
A program may use at most 128 MiB of HBM per device.

```python
import jax
import jax.numpy as jnp
from jax import lax

HEAD_DIM = 128
P_SIZE = 2048
HEADS = 32
FRAMES = 16
TOKENS = 32768


def draw_queries(key, part):
    key = jax.random.fold_in(key, 3)
    shape = (TOKENS, HEADS * HEAD_DIM)
    out = jnp.clip(jax.random.normal(key, shape, jnp.float32), -8.0, 8.0)
    return out.astype(jnp.bfloat16)


def draw_keys(key, part):
    key = jax.random.fold_in(key, 5)
    shape = (TOKENS, HEADS * HEAD_DIM)
    out = jnp.clip(jax.random.normal(key, shape, jnp.float32), -8.0, 8.0)
    return out.astype(jnp.bfloat16)


def plant(drawn, stream_key, least, largest):
    spot = [jax.random.randint(jax.random.fold_in(stream_key, axis), (), 0, length) for axis, length in enumerate(drawn.shape)]
    widest = drawn.shape.index(max(drawn.shape))
    beside = spot[:widest] + [(spot[widest] + 1) % drawn.shape[widest]] + spot[widest + 1:]
    return drawn.at[tuple(spot)].set(least).at[tuple(beside)].set(largest)


def levels(stream_key, shape, pieces, least, top_value):
    level, own = 1.0, jax.random.fold_in(stream_key, 6)
    for dim, shards_of in pieces:
        draws = jnp.exp(jax.random.uniform(jax.random.fold_in(own, dim), (shards_of,), jnp.float32, least / len(pieces), top_value / len(pieces)))
        level = level * jnp.repeat(draws, shape[dim] // shards_of).reshape([-1 if axis == dim else 1 for axis in range(len(shape))])
    return level


def centred(stream_key, dims, width, bound, split=(), held_as=jnp.bfloat16):
    drawn = width * jax.random.normal(stream_key, dims, jnp.float32)
    if split:
        drawn = drawn * levels(stream_key, dims, split, -0.22, 0.18)
    return jnp.clip(drawn, -bound, bound).astype(held_as)


def setup_inputs(seed: int = 0) -> dict:
    key_list = jax.random.split(jax.random.key(seed), 5)
    queries = draw_queries(jax.random.fold_in(key_list[4], 71), 0)
    keys = draw_keys(jax.random.fold_in(key_list[4], 71), 0)
    values = centred(key_list[2], (TOKENS, HEADS * HEAD_DIM), 1.0, 6.0, ((0, 128),))
    head_kind = plant((jax.random.randint(key_list[3], (HEADS,), 0, 2) < 1).astype(jnp.int32), jax.random.fold_in(key_list[3], 1), 0, 1)
    return {"queries": queries, "keys": keys, "values": values, "head_kind": head_kind}


def soft_weights(scores):
    top = jnp.max(scores, axis=-1, keepdims=True)
    expo = jnp.exp(scores - top)
    return (expo / jnp.sum(expo, axis=-1, keepdims=True)).astype(jnp.bfloat16)


def spatial_frame(query_rows, own_keys, own_values, zero_keys, zero_values, first):
    scale = HEAD_DIM ** -0.5
    key_rows = jnp.concatenate([own_keys, zero_keys], axis=0)
    value_rows = jnp.concatenate([own_values, zero_values], axis=0)
    scores = lax.dot_general(query_rows, key_rows, (((1,), (1,)), ((), ())), preferred_element_type=jnp.float32) * scale
    column = jnp.arange(key_rows.shape[0], dtype=jnp.int32)
    hidden_cols = jnp.logical_and(first, column >= own_keys.shape[0])
    scores = jnp.where(hidden_cols[None, :], jnp.float32(-1e30), scores)
    weights = soft_weights(scores)
    return jnp.dot(weights, value_rows, preferred_element_type=jnp.float32).astype(jnp.bfloat16)


def reference(queries, keys, values, head_kind):
    scale = HEAD_DIM ** -0.5

    def split_heads(x):
        return jnp.moveaxis(x.reshape(FRAMES, P_SIZE, HEADS, HEAD_DIM), 2, 0)

    def one_head(args):
        qh, kh, vh, kind = args

        def spatial(unused):
            def per_frame(frame):
                return spatial_frame(qh[frame], kh[frame], vh[frame], kh[0], vh[0], frame == 0)
            return lax.map(per_frame, jnp.arange(FRAMES, dtype=jnp.int32))

        def temporal(unused):
            scores = jnp.einsum("fpd,gpd->pfg", qh.astype(jnp.float32), kh.astype(jnp.float32)) * scale
            weights = soft_weights(scores)
            return jnp.einsum("pfg,gpd->fpd", weights.astype(jnp.float32), vh.astype(jnp.float32)).astype(jnp.bfloat16)

        return lax.cond(kind == 1, temporal, spatial, 0)

    result = lax.map(one_head, (split_heads(queries), split_heads(keys), split_heads(values), head_kind))
    return jnp.moveaxis(result, 0, 2).reshape(TOKENS, HEADS * HEAD_DIM)
```

```python
import functools

import jax
import jax.numpy as jnp
from jax import lax
from jax.experimental import pallas as pl
from jax.experimental.pallas import tpu as pltpu
from jax.sharding import Mesh, PartitionSpec as P

HEAD_DIM = 128
P_SIZE = 2048
HEADS = 32
ROWS = 256
RANKS = 8
FRAMES = 16
SCALE = HEAD_DIM**-0.5
LOG2E = 1.4426950408889634
SAFE = 60.0
FRAME_GROUP = ("yl", "x")
BLOCK_GROUP = ("yh", "yl", "x")
SPOT_GROUP = ("z", "c", "yh")
VMEM = 48 * 1024 * 1024

CASES = ((0, 1, 32), (1, 0, 16), (1, 0, 20), (1, 0, 24), (1, 1, 12), (1, 1, 16), (2, 0, 8))


def order_heads(kind_ref, order_ref):
    spatial = lax.fori_loop(0, HEADS, lambda h, n: n + 1 - kind_ref[h], jnp.int32(0))

    def place(h, counts):
        a, b = counts
        kind = kind_ref[h]
        order_ref[jnp.where(kind == 0, a, b)] = h
        return a + 1 - kind, b + kind

    lax.fori_loop(0, HEADS, place, (jnp.int32(0), spatial))
    return spatial


def columns(slot):
    if isinstance(slot, int):
        return pl.ds(slot * HEAD_DIM, HEAD_DIM)
    return pl.ds(pl.multiple_of(slot * HEAD_DIM, HEAD_DIM), HEAD_DIM)


def pack_s_kernel(width, base, groups, kind_ref, q_ref, k_ref, v_ref, s_ref, order_ref, sems):
    order_heads(kind_ref, order_ref)
    copies = []
    for part, ref in enumerate((q_ref, k_ref, v_ref)):
        for slot in range(groups * width):
            group, place = divmod(slot, width)
            copies.append(
                pltpu.make_async_copy(
                    ref.at[:, columns(order_ref[base + slot])],
                    s_ref.at[group, :, columns(part * width + place)],
                    sems.at[len(copies)],
                )
            )
            copies[-1].start()
    for copy in copies:
        copy.wait()


def pack_s(width, base, groups, head_kind, queries, keys, values):
    return pl.pallas_call(
        functools.partial(pack_s_kernel, width, base, groups),
        out_shape=jax.ShapeDtypeStruct((groups, ROWS, 3 * width * HEAD_DIM), jnp.bfloat16),
        in_specs=[pl.BlockSpec(memory_space=pltpu.SMEM)] + [pl.BlockSpec(memory_space=pl.ANY)] * 3,
        out_specs=pl.BlockSpec(memory_space=pltpu.VMEM),
        scratch_shapes=[
            pltpu.SMEM((HEADS,), jnp.int32),
            pltpu.SemaphoreType.DMA((3 * groups * width,)),
        ],
        compiler_params=pltpu.CompilerParams(vmem_limit_bytes=VMEM),
        name="pack_s",
    )(head_kind, queries, keys, values)


def pack_t_kernel(ct, kind_ref, q_ref, k_ref, v_ref, t_ref, order_ref, sems):
    spatial = order_heads(kind_ref, order_ref)
    copies = []
    for part, ref in enumerate((q_ref, k_ref, v_ref)):
        for slot in range(ct):
            head = order_ref[jnp.minimum(spatial + slot, HEADS - 1)]
            copies.append(
                pltpu.make_async_copy(
                    ref.at[:, columns(head)],
                    t_ref.at[:, columns(part * ct + slot)],
                    sems.at[len(copies)],
                )
            )
            copies[-1].start()
    for copy in copies:
        copy.wait()


def pack_t(ct, head_kind, queries, keys, values):
    return pl.pallas_call(
        functools.partial(pack_t_kernel, ct),
        out_shape=jax.ShapeDtypeStruct((ROWS, 3 * ct * HEAD_DIM), jnp.bfloat16),
        in_specs=[pl.BlockSpec(memory_space=pltpu.SMEM)] + [pl.BlockSpec(memory_space=pl.ANY)] * 3,
        out_specs=pl.BlockSpec(memory_space=pltpu.VMEM),
        scratch_shapes=[
            pltpu.SMEM((HEADS,), jnp.int32),
            pltpu.SemaphoreType.DMA((3 * ct,)),
        ],
        compiler_params=pltpu.CompilerParams(vmem_limit_bytes=VMEM),
        name="pack_t",
    )(head_kind, queries, keys, values)


def unpack_kernel(layouts, ct, kind_ref, *refs):
    s_refs, (t_ref, out_ref, order_ref, sems) = refs[: len(layouts)], refs[len(layouts) :]
    spatial = order_heads(kind_ref, order_ref)
    sources = []
    for (width, base, groups), ref in zip(layouts, s_refs):
        for slot in range(groups * width):
            group, place = divmod(slot, width)
            sources.append(ref.at[group, :, columns(place)])
    waits = []
    for slot in range(HEADS):
        target = out_ref.at[:, columns(order_ref[slot])]
        t_slot = jnp.clip(slot - spatial, 0, ct - 1)
        from_t = pltpu.make_async_copy(t_ref.at[:, columns(t_slot)], target, sems.at[slot])
        pl.when(slot >= spatial)(from_t.start)
        if slot < len(sources):
            from_s = pltpu.make_async_copy(sources[slot], target, sems.at[slot])
            pl.when(slot < spatial)(from_s.start)
        waits.append(from_t)
    for copy in waits:
        copy.wait()


def unpack(layouts, ct, head_kind, s_backs, t_back):
    n = len(layouts)
    return pl.pallas_call(
        functools.partial(unpack_kernel, layouts, ct),
        out_shape=jax.ShapeDtypeStruct((ROWS, HEADS * HEAD_DIM), jnp.bfloat16),
        in_specs=[pl.BlockSpec(memory_space=pltpu.SMEM)]
        + [pl.BlockSpec(memory_space=pltpu.VMEM)] * (n + 1),
        out_specs=pl.BlockSpec(memory_space=pl.ANY),
        scratch_shapes=[pltpu.SMEM((HEADS,), jnp.int32), pltpu.SemaphoreType.DMA((HEADS,))],
        compiler_params=pltpu.CompilerParams(vmem_limit_bytes=VMEM),
        name="unpack",
    )(head_kind, *s_backs, t_back)


def dot_t(a, b):
    return lax.dot_general(a, b, (((1,), (1,)), ((), ())), preferred_element_type=jnp.float32)


def row_norm2(x):
    wide = x.astype(jnp.float32)
    return jnp.max(jnp.sum(wide * wide, axis=-1))


BQ = 512
BK = 512


def spatial_kernel(first_ref, q_ref, k_ref, v_ref, k0_ref, v0_ref, o_ref, vext, knorm):
    @pl.when(pl.program_id(2) == 0)
    def _():
        ones = jnp.ones((P_SIZE, HEAD_DIM), jnp.bfloat16)
        for f, ref in enumerate((v_ref, v0_ref)):
            vext[f, :, :HEAD_DIM] = ref[...].reshape(P_SIZE, HEAD_DIM)
            vext[f, :, HEAD_DIM:] = ones
        knorm[0] = row_norm2(k_ref[...].reshape(P_SIZE, HEAD_DIM))
        knorm[1] = row_norm2(k0_ref[...].reshape(P_SIZE, HEAD_DIM))

    first = jnp.logical_and(first_ref[0] == 1, pl.program_id(1) == 0)
    q = q_ref[...].reshape(BQ, HEAD_DIM)
    kmax = jnp.where(first, knorm[0], jnp.maximum(knorm[0], knorm[1]))
    small = row_norm2(q) * kmax * (SCALE * SCALE) <= SAFE * SAFE
    factor = SCALE * LOG2E

    def key_block(f, b):
        ref = (k_ref, k0_ref)[f]
        if isinstance(b, int):
            return ref[b * (BK // ROWS) : (b + 1) * (BK // ROWS)].reshape(BK, HEAD_DIM)
        return ref[pl.ds(b * (BK // ROWS), BK // ROWS)].reshape(BK, HEAD_DIM)

    def finish(total):
        out = total[:, :HEAD_DIM] / total[:, HEAD_DIM:]
        o_ref[...] = out.astype(jnp.bfloat16).reshape(o_ref.shape)

    def direct(frames):
        total = None
        for f in range(frames):
            for b in range(P_SIZE // BK):
                scores = dot_t(q, key_block(f, b))
                weights = jnp.exp2(scores * factor).astype(jnp.bfloat16)
                term = jnp.dot(
                    weights, vext[f, b * BK : (b + 1) * BK], preferred_element_type=jnp.float32
                )
                total = term if total is None else total + term
        finish(total)

    def with_maximum(frames):
        top = jnp.full((BQ, 1), -jnp.inf, jnp.float32)
        for f in range(frames):

            def highest(b, top):
                scores = dot_t(q, key_block(f, b))
                return jnp.maximum(top, jnp.max(scores, axis=-1, keepdims=True))

            top = lax.fori_loop(0, P_SIZE // BK, highest, top)
        total = jnp.zeros((BQ, 2 * HEAD_DIM), jnp.float32)
        for f in range(frames):

            def add(b, total):
                scores = dot_t(q, key_block(f, b))
                weights = jnp.exp2((scores - top) * factor).astype(jnp.bfloat16)
                rows = vext[f, pl.ds(pl.multiple_of(b * BK, BK), BK)]
                return total + jnp.dot(weights, rows, preferred_element_type=jnp.float32)

            total = lax.fori_loop(0, P_SIZE // BK, add, total)
        finish(total)

    rest = jnp.logical_not(first)
    large = jnp.logical_not(small)
    pl.when(jnp.logical_and(small, rest))(lambda: direct(2))
    pl.when(jnp.logical_and(small, first))(lambda: direct(1))
    pl.when(jnp.logical_and(large, rest))(lambda: with_maximum(2))
    pl.when(jnp.logical_and(large, first))(lambda: with_maximum(1))


def spatial_attention(width, frames, first, qkv, kv0):
    whole = (RANKS, ROWS, HEAD_DIM)
    part = (BQ // ROWS, ROWS, HEAD_DIM)
    steps = P_SIZE // BQ
    grid_spec = pltpu.PrefetchScalarGridSpec(
        num_scalar_prefetch=1,
        grid=(width, frames, steps),
        in_specs=[
            pl.BlockSpec(part, lambda j, u, g, first: (u * steps + g, 0, j)),
            pl.BlockSpec(whole, lambda j, u, g, first: (u, 0, width + j)),
            pl.BlockSpec(whole, lambda j, u, g, first: (u, 0, 2 * width + j)),
            pl.BlockSpec(whole, lambda j, u, g, first: (0, 0, j)),
            pl.BlockSpec(whole, lambda j, u, g, first: (0, 0, width + j)),
        ],
        out_specs=pl.BlockSpec(part, lambda j, u, g, first: (u * steps + g, 0, j)),
        scratch_shapes=[
            pltpu.VMEM((2, P_SIZE, 2 * HEAD_DIM), jnp.bfloat16),
            pltpu.SMEM((2,), jnp.float32),
        ],
    )
    units = width * frames
    return pl.pallas_call(
        spatial_kernel,
        grid_spec=grid_spec,
        out_shape=jax.ShapeDtypeStruct((frames * RANKS, ROWS, width * HEAD_DIM), jnp.bfloat16),
        compiler_params=pltpu.CompilerParams(vmem_limit_bytes=VMEM),
        cost_estimate=pl.CostEstimate(
            flops=units * 2048 * 4096 * 128 * 8,
            bytes_accessed=units * 5 * 2**20,
            transcendentals=units * 2048 * 4096,
        ),
        name="spatial",
    )(first, qkv, qkv, qkv, kv0, kv0)


SPOTS = ROWS // FRAMES
PER_STEP = 4


def temporal_kernel(q_ref, k_ref, v_ref, o_ref):
    row = lax.broadcasted_iota(jnp.int32, (ROWS, ROWS), 0)
    col = lax.broadcasted_iota(jnp.int32, (ROWS, ROWS), 1)
    same = (row & (SPOTS - 1)) == (col & (SPOTS - 1))
    for h in range(PER_STEP):
        cols = slice(h * HEAD_DIM, (h + 1) * HEAD_DIM)
        q, k, v = (ref[:, :, cols].reshape(ROWS, HEAD_DIM) for ref in (q_ref, k_ref, v_ref))
        scores = jnp.where(same, dot_t(q, k) * (SCALE * LOG2E), -1e30)
        top = jnp.max(scores, axis=-1, keepdims=True)
        weights = jnp.exp2(scores - top)
        total = jnp.sum(weights, axis=-1, keepdims=True)
        out = jnp.dot(weights.astype(jnp.bfloat16), v, preferred_element_type=jnp.float32) / total
        o_ref[:, :, cols] = out.astype(jnp.bfloat16).reshape(FRAMES, SPOTS, HEAD_DIM)


def temporal_attention(ct, qkv):
    block = (FRAMES, SPOTS, PER_STEP * HEAD_DIM)
    steps = ct // PER_STEP
    return pl.pallas_call(
        temporal_kernel,
        grid=(steps,),
        in_specs=[
            pl.BlockSpec(block, lambda h: (0, 0, h)),
            pl.BlockSpec(block, lambda h: (0, 0, steps + h)),
            pl.BlockSpec(block, lambda h: (0, 0, 2 * steps + h)),
        ],
        out_specs=pl.BlockSpec(block, lambda h: (0, 0, h)),
        out_shape=jax.ShapeDtypeStruct((FRAMES, SPOTS, ct * HEAD_DIM), jnp.bfloat16),
        compiler_params=pltpu.CompilerParams(vmem_limit_bytes=VMEM),
        cost_estimate=pl.CostEstimate(
            flops=ct * 256 * 256 * 128 * 4,
            bytes_accessed=ct * 2**18,
            transcendentals=ct * 256 * 256,
        ),
        name="temporal",
    )(qkv, qkv, qkv)


def exchange(x, group):
    return lax.all_to_all(x, group, split_axis=0, concat_axis=0, tiled=True)


def spot(z, c, yh):
    return z * 4 + c * 2 + yh


def send(x, pairs):
    return lax.ppermute(x, SPOT_GROUP, [(spot(*a), spot(*b)) for a, b in pairs])


def frame_zero(held, halves):
    z, c, yh = (lax.axis_index(a) for a in SPOT_GROUP)
    ways = [send(held, [((0, 0, h), (i, 0, h)) for h in halves]) for i in (1, 2, 3)]
    ring = jnp.where(z == 0, held, jnp.where(z == 1, ways[0], jnp.where(z == 2, ways[1], ways[2])))
    if len(halves) == 1:
        across = send(ring, [((i, 0, 0), (i, 0, 1)) for i in range(4)])
        ring = jnp.where(yh == 0, ring, across)
    other = send(ring, [((i, 0, j), (i, 1, j)) for i in range(4) for j in range(2)])
    return jnp.where(c == 0, ring, other)


def attend(a, b, ct, queries, keys, values, head_kind):
    z, c, yh = (lax.axis_index(name) for name in SPOT_GROUP)
    layouts = []
    if a:
        layouts.append((a, 0, 2 * RANKS))
    if b:
        layouts.append((b, a * 2 * RANKS, RANKS))
    t_send = pack_t(ct, head_kind, queries, keys, values)
    t_send = t_send.reshape(FRAMES, SPOTS, 3 * ct * HEAD_DIM)
    haves = []
    for width, base, groups in layouts:
        s_send = pack_s(width, base, groups, head_kind, queries, keys, values)
        haves.append(exchange(s_send, BLOCK_GROUP if groups == 2 * RANKS else FRAME_GROUP))
    *haves, t_send = lax.optimization_barrier((*haves, t_send))
    t_have = exchange(t_send, SPOT_GROUP)
    t_out = temporal_attention(ct, t_have)
    backs = []
    for (width, base, groups), have in zip(layouts, haves):
        both = groups == 2 * RANKS
        first = jnp.logical_and(z + c == 0, both or yh == 0)
        first = first.astype(jnp.int32).reshape(1)
        kv0 = frame_zero(have[:RANKS, :, width * HEAD_DIM :], (0, 1) if both else (0,))
        s_out = spatial_attention(width, groups // RANKS, first, have, kv0)
        backs.append(exchange(s_out, BLOCK_GROUP if both else FRAME_GROUP))
    t_back = exchange(t_out, SPOT_GROUP).reshape(ROWS, ct * HEAD_DIM)
    return unpack(layouts, ct, head_kind, backs, t_back)


def on_device(queries, keys, values, head_kind):
    temporal = jnp.sum(head_kind)
    spatial = HEADS - temporal
    index = jnp.int32(len(CASES) - 1)
    for i in reversed(range(len(CASES))):
        a, b, ct = CASES[i]
        room = 2 * RANKS * a + RANKS * b
        index = jnp.where(jnp.logical_and(spatial <= room, temporal <= ct), i, index)
    branches = [functools.partial(attend, *case) for case in CASES]
    return lax.switch(index, branches, queries, keys, values, head_kind)


def solution(mesh):
    fine = Mesh(mesh.devices.reshape(4, 2, 2, 2, 4), ("z", "c", "yh", "yl", "x"))
    rows = P(("z", "c", "yh", "yl", "x"), None)
    return jax.shard_map(
        on_device, mesh=fine, in_specs=(rows, rows, rows, P()), out_specs=rows, check_vma=False
    )
```

```python
import functools

import jax
import jax.numpy as jnp
from jax import lax
from jax.experimental import pallas as pl
from jax.experimental.pallas import tpu as pltpu
from jax.sharding import Mesh, PartitionSpec as P

HEAD_DIM = 128
P_SIZE = 2048
HEADS = 32
ROWS = 256
RANKS = 8
FRAMES = 16
SCALE = HEAD_DIM**-0.5
LOG2E = 1.4426950408889634
SAFE = 60.0
FRAME_GROUP = ("yl", "x")
BLOCK_GROUP = ("yh", "yl", "x")
SPOT_GROUP = ("z", "c", "yh")
VMEM = 48 * 1024 * 1024

CASES = ((1, 0, 20), (1, 1, 16), (1, 0, 32), (2, 0, 8))


def order_heads(kind_ref, order_ref):
    spatial = lax.fori_loop(0, HEADS, lambda h, n: n + 1 - kind_ref[h], jnp.int32(0))

    def place(h, counts):
        a, b = counts
        kind = kind_ref[h]
        order_ref[jnp.where(kind == 0, a, b)] = h
        return a + 1 - kind, b + kind

    lax.fori_loop(0, HEADS, place, (jnp.int32(0), spatial))
    return spatial


def columns(slot):
    if isinstance(slot, int):
        return pl.ds(slot * HEAD_DIM, HEAD_DIM)
    return pl.ds(pl.multiple_of(slot * HEAD_DIM, HEAD_DIM), HEAD_DIM)


def start_columns(part, width, groups, source, target, head_of, sem):
    def each(act):
        @pl.loop(0, groups)
        def _(group):
            for place in range(width):
                head = head_of(place * groups + group)
                copy = pltpu.make_async_copy(
                    source.at[:, columns(head)],
                    target.at[group, :, columns(part * width + place)],
                    sem.at[group * width + place],
                )
                getattr(copy, act)()

    each("start")
    return lambda: each("wait")


def pack_kernel(plan, n_out, kind_ref, q_ref, k_ref, v_ref, *refs):
    outs, order_ref, sems = refs[:n_out], refs[n_out], refs[n_out + 1 :]
    spatial = order_heads(kind_ref, order_ref)
    sources = {"q": q_ref, "k": k_ref, "v": v_ref}
    waits = []
    for sem, (out, part, width, base, groups, name) in zip(sems, plan):

        def head_of(slot, base=base):
            if base is None:
                return order_ref[jnp.minimum(spatial + slot, HEADS - 1)]
            return order_ref[base + slot]

        waits.append(start_columns(part, width, groups, sources[name], outs[out], head_of, sem))
    for wait in waits:
        wait()


def pack(plan, shapes, head_kind, queries, keys, values):
    outs = tuple(jax.ShapeDtypeStruct(shape, jnp.bfloat16) for shape in shapes)
    return pl.pallas_call(
        functools.partial(pack_kernel, plan, len(shapes)),
        out_shape=outs,
        in_specs=[pl.BlockSpec(memory_space=pltpu.SMEM)] + [pl.BlockSpec(memory_space=pl.ANY)] * 3,
        out_specs=(pl.BlockSpec(memory_space=pltpu.VMEM),) * len(shapes),
        scratch_shapes=[pltpu.SMEM((HEADS,), jnp.int32)]
        + [pltpu.SemaphoreType.DMA((width * groups,)) for _, _, width, _, groups, _ in plan],
        compiler_params=pltpu.CompilerParams(vmem_limit_bytes=VMEM),
        name="pack",
    )(head_kind, queries, keys, values)


def unpack_kernel(layouts, ct, kind_ref, *refs):
    s_refs, (t_ref, out_ref, order_ref, sems) = refs[: len(layouts)], refs[len(layouts) :]
    spatial = order_heads(kind_ref, order_ref)

    def target(slot):
        return out_ref.at[:, columns(order_ref[slot])]

    for (width, base, groups), ref in zip(layouts, s_refs):

        @pl.loop(0, groups)
        def _(group):
            for place in range(width):
                slot = base + place * groups + group
                source = ref.at[group, :, columns(place)]
                copy = pltpu.make_async_copy(source, target(slot), sems.at[slot])
                pl.when(slot < spatial)(copy.start)

    def from_t(slot):
        source = t_ref.at[:, columns(jnp.clip(slot - spatial, 0, ct - 1))]
        return pltpu.make_async_copy(source, target(slot), sems.at[slot])

    @pl.loop(spatial, HEADS)
    def _(slot):
        from_t(slot).start()

    @pl.loop(0, HEADS)
    def _(slot):
        from_t(slot).wait()


def unpack(layouts, ct, head_kind, s_backs, t_back):
    n = len(layouts)
    return pl.pallas_call(
        functools.partial(unpack_kernel, layouts, ct),
        out_shape=jax.ShapeDtypeStruct((ROWS, HEADS * HEAD_DIM), jnp.bfloat16),
        in_specs=[pl.BlockSpec(memory_space=pltpu.SMEM)]
        + [pl.BlockSpec(memory_space=pltpu.VMEM)] * (n + 1),
        out_specs=pl.BlockSpec(memory_space=pl.ANY),
        scratch_shapes=[pltpu.SMEM((HEADS,), jnp.int32), pltpu.SemaphoreType.DMA((HEADS,))],
        compiler_params=pltpu.CompilerParams(vmem_limit_bytes=VMEM),
        name="unpack",
    )(head_kind, *s_backs, t_back)


def dot_t(a, b):
    return lax.dot_general(a, b, (((1,), (1,)), ((), ())), preferred_element_type=jnp.float32)


def higher_norm2(best, x):
    wide = x.astype(jnp.float32)
    return jnp.maximum(best, jnp.sum(wide * wide, axis=-1, keepdims=True))


BQ = 1024
STEP = 1024
BK = 256


def spatial_unit(first_ref, q_ref, k_ref, v_ref, k0_ref, v0_ref, o_ref, kext, vext, total, norm):
    first = jnp.logical_and(first_ref[0] == 1, pl.program_id(1) == 0)

    step = pl.program_id(2)
    none = jnp.zeros((ROWS, 1), jnp.float32)

    @pl.when(pl.program_id(0) + pl.program_id(1) + step == 0)
    def _():
        vext[:, HEAD_DIM:] = jnp.ones((2 * P_SIZE, HEAD_DIM), jnp.bfloat16)

    @pl.when(step == 0)
    def _():
        def load(rank, best):
            own = pl.ds(pl.multiple_of(rank * ROWS, ROWS), ROWS)
            zero = pl.ds(pl.multiple_of(P_SIZE + rank * ROWS, ROWS), ROWS)
            kext[own], kext[zero] = k_ref[rank], k0_ref[rank]
            vext[own, :HEAD_DIM], vext[zero, :HEAD_DIM] = v_ref[rank], v0_ref[rank]
            return higher_norm2(higher_norm2(best, k_ref[rank]), k0_ref[rank])

        norm[0] = jnp.max(lax.fori_loop(0, RANKS, load, none))

    q = q_ref[...].reshape(BQ, HEAD_DIM)
    longest = lax.fori_loop(0, BQ // ROWS, lambda i, best: higher_norm2(best, q_ref[i]), none)
    small = norm[0] * jnp.max(longest) * (SCALE * SCALE) <= SAFE * SAFE
    factor = SCALE * LOG2E
    keys = jnp.where(first, P_SIZE, 2 * P_SIZE)

    def block(ref, start, size):
        return ref[pl.ds(pl.multiple_of(start, size), size)]

    total[...] = jnp.zeros_like(total)

    @pl.when(small)
    def _():
        @pl.loop(0, keys // STEP)
        def _(turn):
            for b in range(STEP // BK):
                start = turn * STEP + b * BK
                scores = dot_t(q, block(kext, start, BK))
                weights = jnp.exp2(scores * factor).astype(jnp.bfloat16)
                total[...] += jnp.dot(
                    weights, block(vext, start, BK), preferred_element_type=jnp.float32
                )

    @pl.when(jnp.logical_not(small))
    def _():
        @pl.loop(0, BQ // ROWS)
        def _(part):
            rows = q_ref[part]

            def highest(turn, top):
                scores = dot_t(rows, block(kext, turn * ROWS, ROWS))
                return jnp.maximum(top, jnp.max(scores, axis=-1, keepdims=True))

            lowest = jnp.full((ROWS, 1), -jnp.inf, jnp.float32)
            top = lax.fori_loop(0, keys // ROWS, highest, lowest)

            def add(turn, held):
                scores = dot_t(rows, block(kext, turn * ROWS, ROWS))
                weights = jnp.exp2((scores - top) * factor).astype(jnp.bfloat16)
                values = block(vext, turn * ROWS, ROWS)
                return held + jnp.dot(weights, values, preferred_element_type=jnp.float32)

            held = jnp.zeros((ROWS, 2 * HEAD_DIM), jnp.float32)
            held = lax.fori_loop(0, keys // ROWS, add, held)
            total[pl.ds(pl.multiple_of(part * ROWS, ROWS), ROWS)] = held

    out = total[:, :HEAD_DIM] / total[:, HEAD_DIM:]
    o_ref[...] = out.astype(jnp.bfloat16).reshape(o_ref.shape)


def spatial_kernel(first_ref, *refs):
    pl.when(pl.program_id(0) < first_ref[1])(lambda: spatial_unit(first_ref, *refs))


def spatial_attention(width, frames, first, q, kv, keys_at, kv0):
    whole = (RANKS, ROWS, HEAD_DIM)
    part = (BQ // ROWS, ROWS, HEAD_DIM)
    steps = P_SIZE // BQ
    grid_spec = pltpu.PrefetchScalarGridSpec(
        num_scalar_prefetch=1,
        grid=(width, frames, steps),
        in_specs=[
            pl.BlockSpec(part, lambda j, u, g, first: (u * steps + g, 0, j)),
            pl.BlockSpec(whole, lambda j, u, g, first: (u, 0, keys_at + j)),
            pl.BlockSpec(whole, lambda j, u, g, first: (u, 0, keys_at + width + j)),
            pl.BlockSpec(whole, lambda j, u, g, first: (0, 0, j)),
            pl.BlockSpec(whole, lambda j, u, g, first: (0, 0, j)),
        ],
        out_specs=pl.BlockSpec(part, lambda j, u, g, first: (u * steps + g, 0, j)),
        scratch_shapes=[
            pltpu.VMEM((2 * P_SIZE, HEAD_DIM), jnp.bfloat16),
            pltpu.VMEM((2 * P_SIZE, 2 * HEAD_DIM), jnp.bfloat16),
            pltpu.VMEM((BQ, 2 * HEAD_DIM), jnp.float32),
            pltpu.SMEM((1,), jnp.float32),
        ],
    )
    units = width * frames
    return pl.pallas_call(
        spatial_kernel,
        grid_spec=grid_spec,
        out_shape=jax.ShapeDtypeStruct((frames * RANKS, ROWS, width * HEAD_DIM), jnp.bfloat16),
        compiler_params=pltpu.CompilerParams(vmem_limit_bytes=VMEM),
        cost_estimate=pl.CostEstimate(
            flops=units * 2**26,
            bytes_accessed=units * 2**16,
            transcendentals=units * 2**16,
        ),
        name="spatial",
    )(first, q, kv, kv, *kv0)


SPOTS = ROWS // FRAMES
PER_STEP = 4


def temporal_kernel(q_ref, k_ref, v_ref, o_ref):
    row = lax.broadcasted_iota(jnp.int32, (ROWS, ROWS), 0)
    col = lax.broadcasted_iota(jnp.int32, (ROWS, ROWS), 1)
    same = (row & (SPOTS - 1)) == (col & (SPOTS - 1))
    for h in range(PER_STEP):
        cols = slice(h * HEAD_DIM, (h + 1) * HEAD_DIM)
        q, k, v = (ref[:, :, cols].reshape(ROWS, HEAD_DIM) for ref in (q_ref, k_ref, v_ref))
        scores = jnp.where(same, dot_t(q, k) * (SCALE * LOG2E), -1e30)
        top = jnp.max(scores, axis=-1, keepdims=True)
        weights = jnp.exp2(scores - top)
        total = jnp.sum(weights, axis=-1, keepdims=True)
        out = jnp.dot(weights.astype(jnp.bfloat16), v, preferred_element_type=jnp.float32) / total
        o_ref[:, :, cols] = out.astype(jnp.bfloat16).reshape(FRAMES, SPOTS, HEAD_DIM)


def temporal_attention(ct, qkv):
    block = (FRAMES, SPOTS, PER_STEP * HEAD_DIM)
    steps = ct // PER_STEP
    return pl.pallas_call(
        temporal_kernel,
        grid=(steps,),
        in_specs=[
            pl.BlockSpec(block, lambda h: (0, 0, h)),
            pl.BlockSpec(block, lambda h: (0, 0, steps + h)),
            pl.BlockSpec(block, lambda h: (0, 0, 2 * steps + h)),
        ],
        out_specs=pl.BlockSpec(block, lambda h: (0, 0, h)),
        out_shape=jax.ShapeDtypeStruct((FRAMES, SPOTS, ct * HEAD_DIM), jnp.bfloat16),
        compiler_params=pltpu.CompilerParams(vmem_limit_bytes=VMEM),
        cost_estimate=pl.CostEstimate(
            flops=ct * 256 * 256 * 128 * 4,
            bytes_accessed=ct * 2**18,
            transcendentals=ct * 256 * 256,
        ),
        name="temporal",
    )(qkv, qkv, qkv)


def exchange(x, group):
    return lax.all_to_all(x, group, split_axis=0, concat_axis=0, tiled=True)


def spot(z, c, yh):
    return z * 4 + c * 2 + yh


def send(x, pairs):
    return lax.ppermute(x, SPOT_GROUP, [(spot(*a), spot(*b)) for a, b in pairs])


def along_z(kv, halves):
    z = lax.axis_index("z")
    z1, z3, z2 = (send(kv, [((0, 0, h), (i, 0, h)) for h in halves]) for i in (1, 3, 2))
    return jnp.where(z == 0, kv, jnp.where(z == 1, z1, jnp.where(z == 2, z2, z3)))


def along_y(ring):
    across = send(ring, [((i, 0, 0), (i, 0, 1)) for i in range(4)])
    return jnp.where(lax.axis_index("yh") == 0, ring, across)


def to_core(ring):
    pairs = [((i, 0, h), (i, 1, h)) for i in range(4) for h in range(2)]
    cols = ring.shape[2] // 2
    own = lax.axis_index("c") == 0
    return [jnp.where(own, x, send(x, pairs)) for x in (ring[:, :, :cols], ring[:, :, cols:])]


def attend(a, b, ct, queries, keys, values, head_kind):
    z, c, yh = (lax.axis_index(name) for name in SPOT_GROUP)
    arrays = (head_kind, queries, keys, values)
    wide, narrow = 2 * RANKS, RANKS
    spatial = HEADS - jnp.sum(head_kind)

    def unit(first, base, group, groups, width):
        held = (spatial - base - lax.axis_index(group) + groups - 1) // groups
        return jnp.stack([first.astype(jnp.int32), jnp.clip(held, 0, width)])

    if b:
        base = a * wide
        plan = [(0, part, b, base, narrow, name) for part, name in enumerate("qkv")]
        (qkv_send,) = pack(plan, [(narrow, ROWS, 3 * b * HEAD_DIM)], *arrays)
        qkv_b = exchange(qkv_send, FRAME_GROUP)

    plan = [(0, part, a, 0, wide, name) for part, name in enumerate("kv")]
    (kv_send,) = pack(plan, [(wide, ROWS, 2 * a * HEAD_DIM)], *arrays)
    if b:
        qkv_b, kv_send = lax.optimization_barrier((qkv_b, kv_send))
    kv_a = exchange(kv_send, BLOCK_GROUP)
    if b:
        ring_b = along_y(along_z(qkv_b[:, :, b * HEAD_DIM :], (0,)))

    plan = [(0, 0, a, 0, wide, "q")]
    plan += [(1, part, ct, None, 1, name) for part, name in enumerate("qkv")]
    shapes = [(wide, ROWS, a * HEAD_DIM), (1, ROWS, 3 * ct * HEAD_DIM)]
    q_send, t_send = pack(plan, shapes, *arrays)
    kv_a, q_send = lax.optimization_barrier((kv_a, q_send))
    q_a = exchange(q_send, BLOCK_GROUP)
    ring_a = along_z(kv_a[:RANKS], (0, 1))

    t_send = t_send.reshape(FRAMES, SPOTS, 3 * ct * HEAD_DIM)
    if b:
        q_a, ring_a, ring_b, t_send = lax.optimization_barrier((q_a, ring_a, ring_b, t_send))
    else:
        q_a, ring_a, t_send = lax.optimization_barrier((q_a, ring_a, t_send))
    t_have = exchange(t_send, SPOT_GROUP)

    backs, layouts = [], []
    if b:
        at = unit(z + c + yh == 0, a * wide, FRAME_GROUP, narrow, b)
        out = spatial_attention(b, 1, at, qkv_b, qkv_b, b, to_core(ring_b))
        out, t_have = lax.optimization_barrier((out, t_have))
        backs.append(exchange(out, FRAME_GROUP))
        layouts.append((b, a * wide, narrow))
    at = unit(z + c == 0, 0, BLOCK_GROUP, wide, a)
    out = spatial_attention(a, 2, at, q_a, kv_a, 0, to_core(ring_a))
    backs.append(exchange(out, BLOCK_GROUP))
    layouts.append((a, 0, wide))
    t_out = temporal_attention(ct, t_have)
    t_back = exchange(t_out, SPOT_GROUP).reshape(ROWS, ct * HEAD_DIM)
    return unpack(layouts, ct, head_kind, backs, t_back)


def on_device(queries, keys, values, head_kind):
    temporal = jnp.sum(head_kind)
    spatial = HEADS - temporal
    index = jnp.int32(len(CASES) - 1)
    for i in reversed(range(len(CASES))):
        a, b, ct = CASES[i]
        room = 2 * RANKS * a + RANKS * b
        index = jnp.where(jnp.logical_and(spatial <= room, temporal <= ct), i, index)
    branches = [functools.partial(attend, *case) for case in CASES]
    return lax.switch(index, branches, queries, keys, values, head_kind)


def solution(mesh):
    fine = Mesh(mesh.devices.reshape(4, 2, 2, 2, 4), ("z", "c", "yh", "yl", "x"))
    rows = P(("z", "c", "yh", "yl", "x"), None)
    return jax.shard_map(
        on_device, mesh=fine, in_specs=(rows, rows, rows, P()), out_specs=rows, check_vma=False
    )
```

```python
import functools

import jax
import jax.numpy as jnp
from jax import lax
from jax.experimental import pallas as pl
from jax.experimental.pallas import tpu as pltpu
from jax.sharding import Mesh, PartitionSpec as P

HEAD_DIM = 128
P_SIZE = 2048
HEADS = 32
ROWS = 256
RANKS = 8
FRAMES = 16
SCALE = HEAD_DIM**-0.5
LOG2E = 1.4426950408889634
SAFE = 60.0
FRAME_GROUP = ("yl", "x")
BLOCK_GROUP = ("yh", "yl", "x")
SPOT_GROUP = ("z", "c", "yh")
VMEM = 48 * 1024 * 1024

CASES = ((1, 0, 20), (1, 1, 16), (2, 0, 32))


def order_heads(kind_ref, order_ref):
    spatial = lax.fori_loop(0, HEADS, lambda h, n: n + 1 - kind_ref[h], jnp.int32(0))

    def place(h, counts):
        a, b = counts
        kind = kind_ref[h]
        order_ref[jnp.where(kind == 0, a, b)] = h
        return a + 1 - kind, b + kind

    lax.fori_loop(0, HEADS, place, (jnp.int32(0), spatial))
    return spatial


def columns(slot):
    if isinstance(slot, int):
        return pl.ds(slot * HEAD_DIM, HEAD_DIM)
    return pl.ds(pl.multiple_of(slot * HEAD_DIM, HEAD_DIM), HEAD_DIM)


def start_columns(part, width, groups, source, target, head_of, sem):
    def each(act):
        @pl.loop(0, groups)
        def _(group):
            for place in range(width):
                head = head_of(place * groups + group)
                copy = pltpu.make_async_copy(
                    source.at[:, columns(head)],
                    target.at[group, :, columns(part * width + place)],
                    sem.at[group * width + place],
                )
                getattr(copy, act)()

    each("start")
    return lambda: each("wait")


def pack_kernel(plan, n_out, kind_ref, q_ref, k_ref, v_ref, *refs):
    outs, order_ref, sems = refs[:n_out], refs[n_out], refs[n_out + 1 :]
    spatial = order_heads(kind_ref, order_ref)
    sources = {"q": q_ref, "k": k_ref, "v": v_ref}
    waits = []
    for sem, (out, part, width, base, groups, name) in zip(sems, plan):

        def head_of(slot, base=base):
            if base is None:
                return order_ref[jnp.minimum(spatial + slot, HEADS - 1)]
            return order_ref[base + slot]

        waits.append(start_columns(part, width, groups, sources[name], outs[out], head_of, sem))
    for wait in waits:
        wait()


def pack(plan, shapes, head_kind, queries, keys, values):
    outs = tuple(jax.ShapeDtypeStruct(shape, jnp.bfloat16) for shape in shapes)
    return pl.pallas_call(
        functools.partial(pack_kernel, plan, len(shapes)),
        out_shape=outs,
        in_specs=[pl.BlockSpec(memory_space=pltpu.SMEM)] + [pl.BlockSpec(memory_space=pl.ANY)] * 3,
        out_specs=(pl.BlockSpec(memory_space=pltpu.VMEM),) * len(shapes),
        scratch_shapes=[pltpu.SMEM((HEADS,), jnp.int32)]
        + [pltpu.SemaphoreType.DMA((width * groups,)) for _, _, width, _, groups, _ in plan],
        compiler_params=pltpu.CompilerParams(vmem_limit_bytes=VMEM),
        name="pack",
    )(head_kind, queries, keys, values)


def unpack_kernel(layouts, ct, kind_ref, *refs):
    s_refs, (t_ref, out_ref, order_ref, sems) = refs[: len(layouts)], refs[len(layouts) :]
    spatial = order_heads(kind_ref, order_ref)

    def target(slot):
        return out_ref.at[:, columns(order_ref[slot])]

    for (width, base, groups), ref in zip(layouts, s_refs):

        @pl.loop(0, groups)
        def _(group):
            for place in range(width):
                slot = base + place * groups + group
                source = ref.at[group, :, columns(place)]
                copy = pltpu.make_async_copy(source, target(slot), sems.at[slot])
                pl.when(slot < spatial)(copy.start)

    def from_t(slot):
        source = t_ref.at[:, columns(jnp.clip(slot - spatial, 0, ct - 1))]
        return pltpu.make_async_copy(source, target(slot), sems.at[slot])

    @pl.loop(spatial, HEADS)
    def _(slot):
        from_t(slot).start()

    @pl.loop(0, HEADS)
    def _(slot):
        from_t(slot).wait()


def unpack(layouts, ct, head_kind, s_backs, t_back):
    n = len(layouts)
    return pl.pallas_call(
        functools.partial(unpack_kernel, layouts, ct),
        out_shape=jax.ShapeDtypeStruct((ROWS, HEADS * HEAD_DIM), jnp.bfloat16),
        in_specs=[pl.BlockSpec(memory_space=pltpu.SMEM)]
        + [pl.BlockSpec(memory_space=pltpu.VMEM)] * (n + 1),
        out_specs=pl.BlockSpec(memory_space=pl.ANY),
        scratch_shapes=[pltpu.SMEM((HEADS,), jnp.int32), pltpu.SemaphoreType.DMA((HEADS,))],
        compiler_params=pltpu.CompilerParams(vmem_limit_bytes=VMEM),
        name="unpack",
    )(head_kind, *s_backs, t_back)


def dot_t(a, b):
    return lax.dot_general(a, b, (((1,), (1,)), ((), ())), preferred_element_type=jnp.float32)


def higher_norm2(best, x):
    wide = x.astype(jnp.float32)
    return jnp.maximum(best, jnp.sum(wide * wide, axis=-1, keepdims=True))


BQ = 1024
STEP = 1024
BK = 256


def spatial_unit(first_ref, q_ref, k_ref, v_ref, k0_ref, v0_ref, o_ref, kext, vext, total, norm):
    first = jnp.logical_and(first_ref[0] == 1, pl.program_id(1) == 0)

    step = pl.program_id(2)
    none = jnp.zeros((ROWS, 1), jnp.float32)

    @pl.when(pl.program_id(0) + pl.program_id(1) + step == 0)
    def _():
        vext[:, HEAD_DIM:] = jnp.ones((2 * P_SIZE, HEAD_DIM), jnp.bfloat16)

    @pl.when(step == 0)
    def _():
        def load(rank, best):
            own = pl.ds(pl.multiple_of(rank * ROWS, ROWS), ROWS)
            zero = pl.ds(pl.multiple_of(P_SIZE + rank * ROWS, ROWS), ROWS)
            kext[own], kext[zero] = k_ref[rank], k0_ref[rank]
            vext[own, :HEAD_DIM], vext[zero, :HEAD_DIM] = v_ref[rank], v0_ref[rank]
            return higher_norm2(higher_norm2(best, k_ref[rank]), k0_ref[rank])

        norm[0] = jnp.max(lax.fori_loop(0, RANKS, load, none))

    q = q_ref[...].reshape(BQ, HEAD_DIM)
    longest = lax.fori_loop(0, BQ // ROWS, lambda i, best: higher_norm2(best, q_ref[i]), none)
    small = norm[0] * jnp.max(longest) * (SCALE * SCALE) <= SAFE * SAFE
    factor = SCALE * LOG2E
    keys = jnp.where(first, P_SIZE, 2 * P_SIZE)

    def block(ref, start, size):
        return ref[pl.ds(pl.multiple_of(start, size), size)]

    total[...] = jnp.zeros_like(total)

    @pl.when(small)
    def _():
        @pl.loop(0, keys // STEP)
        def _(turn):
            for b in range(STEP // BK):
                start = turn * STEP + b * BK
                scores = dot_t(q, block(kext, start, BK))
                weights = jnp.exp2(scores * factor).astype(jnp.bfloat16)
                total[...] += jnp.dot(
                    weights, block(vext, start, BK), preferred_element_type=jnp.float32
                )

    @pl.when(jnp.logical_not(small))
    def _():
        @pl.loop(0, BQ // ROWS)
        def _(part):
            rows = q_ref[part]

            def highest(turn, top):
                scores = dot_t(rows, block(kext, turn * ROWS, ROWS))
                return jnp.maximum(top, jnp.max(scores, axis=-1, keepdims=True))

            lowest = jnp.full((ROWS, 1), -jnp.inf, jnp.float32)
            top = lax.fori_loop(0, keys // ROWS, highest, lowest)

            def add(turn, held):
                scores = dot_t(rows, block(kext, turn * ROWS, ROWS))
                weights = jnp.exp2((scores - top) * factor).astype(jnp.bfloat16)
                values = block(vext, turn * ROWS, ROWS)
                return held + jnp.dot(weights, values, preferred_element_type=jnp.float32)

            held = jnp.zeros((ROWS, 2 * HEAD_DIM), jnp.float32)
            held = lax.fori_loop(0, keys // ROWS, add, held)
            total[pl.ds(pl.multiple_of(part * ROWS, ROWS), ROWS)] = held

    out = total[:, :HEAD_DIM] / total[:, HEAD_DIM:]
    o_ref[...] = out.astype(jnp.bfloat16).reshape(o_ref.shape)


def spatial_kernel(first_ref, *refs):
    pl.when(pl.program_id(0) < first_ref[1])(lambda: spatial_unit(first_ref, *refs))


def spatial_attention(width, frames, first, q, kv, keys_at, kv0):
    whole = (RANKS, ROWS, HEAD_DIM)
    part = (BQ // ROWS, ROWS, HEAD_DIM)
    steps = P_SIZE // BQ
    grid_spec = pltpu.PrefetchScalarGridSpec(
        num_scalar_prefetch=1,
        grid=(width, frames, steps),
        in_specs=[
            pl.BlockSpec(part, lambda j, u, g, first: (u * steps + g, 0, j)),
            pl.BlockSpec(whole, lambda j, u, g, first: (u, 0, keys_at + j)),
            pl.BlockSpec(whole, lambda j, u, g, first: (u, 0, keys_at + width + j)),
            pl.BlockSpec(whole, lambda j, u, g, first: (0, 0, j)),
            pl.BlockSpec(whole, lambda j, u, g, first: (0, 0, width + j)),
        ],
        out_specs=pl.BlockSpec(part, lambda j, u, g, first: (u * steps + g, 0, j)),
        scratch_shapes=[
            pltpu.VMEM((2 * P_SIZE, HEAD_DIM), jnp.bfloat16),
            pltpu.VMEM((2 * P_SIZE, 2 * HEAD_DIM), jnp.bfloat16),
            pltpu.VMEM((BQ, 2 * HEAD_DIM), jnp.float32),
            pltpu.SMEM((1,), jnp.float32),
        ],
    )
    units = width * frames
    return pl.pallas_call(
        spatial_kernel,
        grid_spec=grid_spec,
        out_shape=jax.ShapeDtypeStruct((frames * RANKS, ROWS, width * HEAD_DIM), jnp.bfloat16),
        compiler_params=pltpu.CompilerParams(vmem_limit_bytes=VMEM),
        cost_estimate=pl.CostEstimate(
            flops=units * 2**26,
            bytes_accessed=units * 2**16,
            transcendentals=units * 2**16,
        ),
        name="spatial",
    )(first, q, kv, kv, kv0, kv0)


SPOTS = ROWS // FRAMES
PER_STEP = 4


def temporal_kernel(q_ref, k_ref, v_ref, o_ref):
    row = lax.broadcasted_iota(jnp.int32, (ROWS, ROWS), 0)
    col = lax.broadcasted_iota(jnp.int32, (ROWS, ROWS), 1)
    same = (row & (SPOTS - 1)) == (col & (SPOTS - 1))
    for h in range(PER_STEP):
        cols = slice(h * HEAD_DIM, (h + 1) * HEAD_DIM)
        q, k, v = (ref[:, :, cols].reshape(ROWS, HEAD_DIM) for ref in (q_ref, k_ref, v_ref))
        scores = jnp.where(same, dot_t(q, k) * (SCALE * LOG2E), -1e30)
        top = jnp.max(scores, axis=-1, keepdims=True)
        weights = jnp.exp2(scores - top)
        total = jnp.sum(weights, axis=-1, keepdims=True)
        out = jnp.dot(weights.astype(jnp.bfloat16), v, preferred_element_type=jnp.float32) / total
        o_ref[:, :, cols] = out.astype(jnp.bfloat16).reshape(FRAMES, SPOTS, HEAD_DIM)


def temporal_attention(ct, qkv):
    block = (FRAMES, SPOTS, PER_STEP * HEAD_DIM)
    steps = ct // PER_STEP
    return pl.pallas_call(
        temporal_kernel,
        grid=(steps,),
        in_specs=[
            pl.BlockSpec(block, lambda h: (0, 0, h)),
            pl.BlockSpec(block, lambda h: (0, 0, steps + h)),
            pl.BlockSpec(block, lambda h: (0, 0, 2 * steps + h)),
        ],
        out_specs=pl.BlockSpec(block, lambda h: (0, 0, h)),
        out_shape=jax.ShapeDtypeStruct((FRAMES, SPOTS, ct * HEAD_DIM), jnp.bfloat16),
        compiler_params=pltpu.CompilerParams(vmem_limit_bytes=VMEM),
        cost_estimate=pl.CostEstimate(
            flops=ct * 256 * 256 * 128 * 4,
            bytes_accessed=ct * 2**18,
            transcendentals=ct * 256 * 256,
        ),
        name="temporal",
    )(qkv, qkv, qkv)


def exchange(x, group):
    return lax.all_to_all(x, group, split_axis=0, concat_axis=0, tiled=True)


def spot(z, c, yh):
    return z * 4 + c * 2 + yh


def send(x, pairs):
    return lax.ppermute(x, SPOT_GROUP, [(spot(*a), spot(*b)) for a, b in pairs])


def along_z(kv, halves):
    z = lax.axis_index("z")
    z1, z3, z2 = (send(kv, [((0, 0, h), (i, 0, h)) for h in halves]) for i in (1, 3, 2))
    return jnp.where(z == 0, kv, jnp.where(z == 1, z1, jnp.where(z == 2, z2, z3)))


def along_y(ring):
    across = send(ring, [((i, 0, 0), (i, 0, 1)) for i in range(4)])
    return jnp.where(lax.axis_index("yh") == 0, ring, across)


def to_core(ring):
    pairs = [((i, 0, h), (i, 1, h)) for i in range(4) for h in range(2)]
    return jnp.where(lax.axis_index("c") == 0, ring, send(ring, pairs))


def along(x, axis, step):
    return lax.ppermute(x, axis, [(i, (i + step) % 4) for i in range(4)])


Y_AXIS = ("yh", "yl")


def place_x():
    return lax.axis_index("x")


def place_y():
    return lax.axis_index("yh") * 2 + lax.axis_index("yl")


def run_copies(copies):
    for copy in copies:
        copy.start()
    for copy in copies:
        copy.wait()


def shuffle(kernel, outs, n_copies, name, *args):
    return pl.pallas_call(
        kernel,
        out_shape=tuple(jax.ShapeDtypeStruct(shape, jnp.bfloat16) for shape in outs),
        in_specs=[pl.BlockSpec(memory_space=pl.ANY)] * len(args),
        out_specs=(pl.BlockSpec(memory_space=pltpu.VMEM),) * len(outs),
        scratch_shapes=[pltpu.SemaphoreType.DMA((n_copies,))],
        compiler_params=pltpu.CompilerParams(vmem_limit_bytes=VMEM),
        name=name,
    )(*args)


def pick_kernel(ref, *refs):
    outs, sems = refs[:4], refs[4]
    y = place_y()
    run_copies(
        [
            pltpu.make_async_copy(ref.at[pl.ds((y + step) % 4 * 4, 4)], out, sems.at[step])
            for step, out in enumerate(outs)
        ]
    )


def turn_kernel(*refs):
    ins, outs, sems = refs[:4], refs[4:8], refs[8]
    x, y = place_x(), place_y()
    run_copies(
        [
            pltpu.make_async_copy(
                ref.at[(x + step) % 4], out.at[(y + 4 - back) % 4], sems.at[4 * step + back]
            )
            for step, out in enumerate(outs)
            for back, ref in enumerate(ins)
        ]
    )


def settle_kernel(*refs):
    ins, out, sems = refs[:4], refs[4], refs[5]
    x = place_x()
    run_copies(
        [
            pltpu.make_async_copy(
                ref.at[y], out.at[4 * y + (x + 4 - back) % 4], sems.at[4 * back + y]
            )
            for back, ref in enumerate(ins)
            for y in range(4)
        ]
    )


def attend(a, b, ct, queries, keys, values, head_kind):
    z, c, yh = (lax.axis_index(name) for name in SPOT_GROUP)
    arrays = (head_kind, queries, keys, values)
    wide, narrow = 2 * RANKS, RANKS
    spatial = HEADS - jnp.sum(head_kind)

    def unit(first, base, group, groups, width):
        held = (spatial - base - lax.axis_index(group) + groups - 1) // groups
        return jnp.stack([first.astype(jnp.int32), jnp.clip(held, 0, width)])

    if b:
        base = a * wide
        plan = [(0, part, b, base, narrow, name) for part, name in enumerate("qkv")]
        (qkv_send,) = pack(plan, [(narrow, ROWS, 3 * b * HEAD_DIM)], *arrays)
        qkv_b = exchange(qkv_send, FRAME_GROUP)

    plan = [(0, part, a, 0, wide, name) for part, name in enumerate("kv")]
    (kv_send,) = pack(plan, [(wide, ROWS, 2 * a * HEAD_DIM)], *arrays)
    plan = [(0, 0, a, 0, wide, "q")]
    plan += [(1, part, ct, None, 1, name) for part, name in enumerate("qkv")]
    shapes = [(wide, ROWS, a * HEAD_DIM), (1, ROWS, 3 * ct * HEAD_DIM)]
    q_send, t_send = pack(plan, shapes, *arrays)
    if b:
        qkv_b, kv_send, q_send, t_send = lax.optimization_barrier((qkv_b, kv_send, q_send, t_send))
    kv_a = exchange(kv_send, BLOCK_GROUP)
    if b:
        zero_b = to_core(along_y(along_z(qkv_b[:, :, b * HEAD_DIM :], (0,))))

    kv_a, q_send = lax.optimization_barrier((kv_a, q_send))
    q_a = exchange(q_send, BLOCK_GROUP)
    ring_a = along_z(kv_a[:RANKS], (0, 1))

    t_send = t_send.reshape(FRAMES, SPOTS, 3 * ct * HEAD_DIM)
    if b:
        q_a, ring_a, zero_b, t_send = lax.optimization_barrier((q_a, ring_a, zero_b, t_send))
    else:
        q_a, ring_a, t_send = lax.optimization_barrier((q_a, ring_a, t_send))
    t_have = exchange(t_send, SPOT_GROUP)

    at = unit(z + c == 0, 0, BLOCK_GROUP, wide, a)
    layouts = [(a, 0, wide)]
    if b:
        at_b = unit(z + c + yh == 0, a * wide, FRAME_GROUP, narrow, b)
        out_b = spatial_attention(b, 1, at_b, qkv_b, qkv_b, b, zero_b)
        q_a, out_b = lax.optimization_barrier((q_a, out_b))
        out = spatial_attention(a, 2, at, q_a, kv_a, 0, to_core(ring_a))
        out_b, out, t_have = lax.optimization_barrier((out_b, out, t_have))
        back_b = exchange(out_b, FRAME_GROUP)
        out, back_b = lax.optimization_barrier((out, back_b))
        layouts.append((b, a * wide, narrow))
        backs = [exchange(out, BLOCK_GROUP), back_b]
        t_out = temporal_attention(ct, t_have)
    else:
        out = spatial_attention(a, 2, at, q_a, kv_a, 0, to_core(ring_a))
        part = [(4, ROWS, a * HEAD_DIM)] * 4
        to_y = shuffle(pick_kernel, part, 4, "pick", out)
        on_y = [to_y[0]] + [along(to_y[step], Y_AXIS, step) for step in (1, 2, 3)]
        t_have = lax.optimization_barrier((t_have, to_y))[0]
        t_out = temporal_attention(ct, t_have)
        on_y, t_out = lax.optimization_barrier((on_y, t_out))
        to_x = shuffle(turn_kernel, part, 16, "turn", *on_y)
        t_out, to_x = lax.optimization_barrier((t_out, to_x))
        on_x = [to_x[0]] + [along(to_x[step], "x", step) for step in (1, 2, 3)]
        backs = shuffle(settle_kernel, [(16, ROWS, a * HEAD_DIM)], 16, "settle", *on_x)
    t_back = exchange(t_out, SPOT_GROUP).reshape(ROWS, ct * HEAD_DIM)
    return unpack(layouts, ct, head_kind, backs, t_back)


def on_device(queries, keys, values, head_kind):
    temporal = jnp.sum(head_kind)
    spatial = HEADS - temporal
    index = jnp.int32(len(CASES) - 1)
    for i in reversed(range(len(CASES))):
        a, b, ct = CASES[i]
        room = 2 * RANKS * a + RANKS * b
        index = jnp.where(jnp.logical_and(spatial <= room, temporal <= ct), i, index)
    branches = [functools.partial(attend, *case) for case in CASES]
    return lax.switch(index, branches, queries, keys, values, head_kind)


def solution(mesh):
    fine = Mesh(mesh.devices.reshape(4, 2, 2, 2, 4), ("z", "c", "yh", "yl", "x"))
    rows = P(("z", "c", "yh", "yl", "x"), None)
    return jax.shard_map(
        on_device, mesh=fine, in_specs=(rows, rows, rows, P()), out_specs=rows, check_vma=False
    )
```

```python
import functools

import jax
import jax.numpy as jnp
from jax import lax
from jax.experimental import pallas as pl
from jax.experimental.pallas import tpu as pltpu
from jax.sharding import Mesh, PartitionSpec as P

HEAD_DIM = 128
P_SIZE = 2048
HEADS = 32
ROWS = 256
RANKS = 8
FRAMES = 16
SCALE = HEAD_DIM**-0.5
LOG2E = 1.4426950408889634
SAFE = 60.0
FRAME_GROUP = ("yl", "x")
BLOCK_GROUP = ("yh", "yl", "x")
SPOT_GROUP = ("z", "c", "yh")
VMEM = 48 * 1024 * 1024

CASES = ((1, 0, 20), (1, 1, 16), (2, 0, 32))


def order_heads(kind_ref, order_ref):
    spatial = lax.fori_loop(0, HEADS, lambda h, n: n + 1 - kind_ref[h], jnp.int32(0))

    def place(h, counts):
        a, b = counts
        kind = kind_ref[h]
        order_ref[jnp.where(kind == 0, a, b)] = h
        return a + 1 - kind, b + kind

    lax.fori_loop(0, HEADS, place, (jnp.int32(0), spatial))
    return spatial


def columns(slot):
    if isinstance(slot, int):
        return pl.ds(slot * HEAD_DIM, HEAD_DIM)
    return pl.ds(pl.multiple_of(slot * HEAD_DIM, HEAD_DIM), HEAD_DIM)


def start_columns(part, width, groups, source, target, head_of, sem):
    def each(act):
        @pl.loop(0, groups)
        def _(group):
            for place in range(width):
                head = head_of(place * groups + group)
                copy = pltpu.make_async_copy(
                    source.at[:, columns(head)],
                    target.at[group, :, columns(part * width + place)],
                    sem.at[group * width + place],
                )
                getattr(copy, act)()

    each("start")
    return lambda: each("wait")


def pack_kernel(plan, n_out, kind_ref, q_ref, k_ref, v_ref, *refs):
    outs, order_ref, sems = refs[:n_out], refs[n_out], refs[n_out + 1 :]
    spatial = order_heads(kind_ref, order_ref)
    sources = {"q": q_ref, "k": k_ref, "v": v_ref}
    waits = []
    for sem, (out, part, width, base, groups, name) in zip(sems, plan):

        def head_of(slot, base=base):
            if base is None:
                return order_ref[jnp.minimum(spatial + slot, HEADS - 1)]
            return order_ref[base + slot]

        waits.append(start_columns(part, width, groups, sources[name], outs[out], head_of, sem))
    for wait in waits:
        wait()


def pack(plan, shapes, head_kind, queries, keys, values):
    outs = tuple(jax.ShapeDtypeStruct(shape, jnp.bfloat16) for shape in shapes)
    return pl.pallas_call(
        functools.partial(pack_kernel, plan, len(shapes)),
        out_shape=outs,
        in_specs=[pl.BlockSpec(memory_space=pltpu.SMEM)] + [pl.BlockSpec(memory_space=pl.ANY)] * 3,
        out_specs=(pl.BlockSpec(memory_space=pltpu.VMEM),) * len(shapes),
        scratch_shapes=[pltpu.SMEM((HEADS,), jnp.int32)]
        + [pltpu.SemaphoreType.DMA((width * groups,)) for _, _, width, _, groups, _ in plan],
        compiler_params=pltpu.CompilerParams(vmem_limit_bytes=VMEM),
        name="pack",
    )(head_kind, queries, keys, values)


def unpack_kernel(layouts, ct, kind_ref, *refs):
    s_refs, (t_ref, out_ref, order_ref, sems) = refs[: len(layouts)], refs[len(layouts) :]
    spatial = order_heads(kind_ref, order_ref)

    def target(slot):
        return out_ref.at[:, columns(order_ref[slot])]

    for (width, base, groups), ref in zip(layouts, s_refs):

        @pl.loop(0, groups)
        def _(group):
            for place in range(width):
                slot = base + place * groups + group
                source = ref.at[group, :, columns(place)]
                copy = pltpu.make_async_copy(source, target(slot), sems.at[slot])
                pl.when(slot < spatial)(copy.start)

    def from_t(slot):
        source = t_ref.at[:, columns(jnp.clip(slot - spatial, 0, ct - 1))]
        return pltpu.make_async_copy(source, target(slot), sems.at[slot])

    @pl.loop(spatial, HEADS)
    def _(slot):
        from_t(slot).start()

    @pl.loop(0, HEADS)
    def _(slot):
        from_t(slot).wait()


def unpack(layouts, ct, head_kind, s_backs, t_back):
    n = len(layouts)
    return pl.pallas_call(
        functools.partial(unpack_kernel, layouts, ct),
        out_shape=jax.ShapeDtypeStruct((ROWS, HEADS * HEAD_DIM), jnp.bfloat16),
        in_specs=[pl.BlockSpec(memory_space=pltpu.SMEM)]
        + [pl.BlockSpec(memory_space=pltpu.VMEM)] * (n + 1),
        out_specs=pl.BlockSpec(memory_space=pl.ANY),
        scratch_shapes=[pltpu.SMEM((HEADS,), jnp.int32), pltpu.SemaphoreType.DMA((HEADS,))],
        compiler_params=pltpu.CompilerParams(vmem_limit_bytes=VMEM),
        name="unpack",
    )(head_kind, *s_backs, t_back)


def dot_t(a, b):
    return lax.dot_general(a, b, (((1,), (1,)), ((), ())), preferred_element_type=jnp.float32)


def higher_norm2(best, x):
    wide = x.astype(jnp.float32)
    return jnp.maximum(best, jnp.sum(wide * wide, axis=-1, keepdims=True))


BQ = 1024
STEP = 1024
BK = 256


def spatial_unit(first_ref, q_ref, k_ref, v_ref, k0_ref, v0_ref, o_ref, kext, vext, total, norm):
    first = jnp.logical_and(first_ref[0] == 1, pl.program_id(1) == 0)

    step = pl.program_id(2)
    none = jnp.zeros((ROWS, 1), jnp.float32)

    @pl.when(pl.program_id(0) + pl.program_id(1) + step == 0)
    def _():
        vext[:, HEAD_DIM:] = jnp.ones((2 * P_SIZE, HEAD_DIM), jnp.bfloat16)

    @pl.when(step == 0)
    def _():
        def load(rank, best):
            own = pl.ds(pl.multiple_of(rank * ROWS, ROWS), ROWS)
            zero = pl.ds(pl.multiple_of(P_SIZE + rank * ROWS, ROWS), ROWS)
            kext[own], kext[zero] = k_ref[rank], k0_ref[rank]
            vext[own, :HEAD_DIM], vext[zero, :HEAD_DIM] = v_ref[rank], v0_ref[rank]
            return higher_norm2(higher_norm2(best, k_ref[rank]), k0_ref[rank])

        norm[0] = jnp.max(lax.fori_loop(0, RANKS, load, none))

    q = q_ref[...].reshape(BQ, HEAD_DIM)
    longest = lax.fori_loop(0, BQ // ROWS, lambda i, best: higher_norm2(best, q_ref[i]), none)
    small = norm[0] * jnp.max(longest) * (SCALE * SCALE) <= SAFE * SAFE
    factor = SCALE * LOG2E
    keys = jnp.where(first, P_SIZE, 2 * P_SIZE)

    def block(ref, start, size):
        return ref[pl.ds(pl.multiple_of(start, size), size)]

    total[...] = jnp.zeros_like(total)

    @pl.when(small)
    def _():
        @pl.loop(0, keys // STEP)
        def _(turn):
            for b in range(STEP // BK):
                start = turn * STEP + b * BK
                scores = dot_t(q, block(kext, start, BK))
                weights = jnp.exp2(scores * factor).astype(jnp.bfloat16)
                total[...] += jnp.dot(
                    weights, block(vext, start, BK), preferred_element_type=jnp.float32
                )

    @pl.when(jnp.logical_not(small))
    def _():
        @pl.loop(0, BQ // ROWS)
        def _(part):
            rows = q_ref[part]

            def highest(turn, top):
                scores = dot_t(rows, block(kext, turn * ROWS, ROWS))
                return jnp.maximum(top, jnp.max(scores, axis=-1, keepdims=True))

            lowest = jnp.full((ROWS, 1), -jnp.inf, jnp.float32)
            top = lax.fori_loop(0, keys // ROWS, highest, lowest)

            def add(turn, held):
                scores = dot_t(rows, block(kext, turn * ROWS, ROWS))
                weights = jnp.exp2((scores - top) * factor).astype(jnp.bfloat16)
                values = block(vext, turn * ROWS, ROWS)
                return held + jnp.dot(weights, values, preferred_element_type=jnp.float32)

            held = jnp.zeros((ROWS, 2 * HEAD_DIM), jnp.float32)
            held = lax.fori_loop(0, keys // ROWS, add, held)
            total[pl.ds(pl.multiple_of(part * ROWS, ROWS), ROWS)] = held

    out = total[:, :HEAD_DIM] / total[:, HEAD_DIM:]
    o_ref[...] = out.astype(jnp.bfloat16).reshape(o_ref.shape)


def spatial_kernel(first_ref, *refs):
    pl.when(pl.program_id(0) < first_ref[1])(lambda: spatial_unit(first_ref, *refs))


def spatial_attention(width, frames, first, q, kv, keys_at, kv0):
    whole = (RANKS, ROWS, HEAD_DIM)
    part = (BQ // ROWS, ROWS, HEAD_DIM)
    steps = P_SIZE // BQ
    grid_spec = pltpu.PrefetchScalarGridSpec(
        num_scalar_prefetch=1,
        grid=(width, frames, steps),
        in_specs=[
            pl.BlockSpec(part, lambda j, u, g, first: (u * steps + g, 0, j)),
            pl.BlockSpec(whole, lambda j, u, g, first: (u, 0, keys_at + j)),
            pl.BlockSpec(whole, lambda j, u, g, first: (u, 0, keys_at + width + j)),
            pl.BlockSpec(whole, lambda j, u, g, first: (0, 0, j)),
            pl.BlockSpec(whole, lambda j, u, g, first: (0, 0, width + j)),
        ],
        out_specs=pl.BlockSpec(part, lambda j, u, g, first: (u * steps + g, 0, j)),
        scratch_shapes=[
            pltpu.VMEM((2 * P_SIZE, HEAD_DIM), jnp.bfloat16),
            pltpu.VMEM((2 * P_SIZE, 2 * HEAD_DIM), jnp.bfloat16),
            pltpu.VMEM((BQ, 2 * HEAD_DIM), jnp.float32),
            pltpu.SMEM((1,), jnp.float32),
        ],
    )
    units = width * frames
    return pl.pallas_call(
        spatial_kernel,
        grid_spec=grid_spec,
        out_shape=jax.ShapeDtypeStruct((frames * RANKS, ROWS, width * HEAD_DIM), jnp.bfloat16),
        compiler_params=pltpu.CompilerParams(vmem_limit_bytes=VMEM),
        cost_estimate=pl.CostEstimate(
            flops=units * 2**26,
            bytes_accessed=units * 2**16,
            transcendentals=units * 2**16,
        ),
        name="spatial",
    )(first, q, kv, kv, kv0, kv0)


SPOTS = ROWS // FRAMES
PER_STEP = 4


def temporal_kernel(q_ref, k_ref, v_ref, o_ref):
    row = lax.broadcasted_iota(jnp.int32, (ROWS, ROWS), 0)
    col = lax.broadcasted_iota(jnp.int32, (ROWS, ROWS), 1)
    same = (row & (SPOTS - 1)) == (col & (SPOTS - 1))
    for h in range(PER_STEP):
        cols = slice(h * HEAD_DIM, (h + 1) * HEAD_DIM)
        q, k, v = (ref[:, :, cols].reshape(ROWS, HEAD_DIM) for ref in (q_ref, k_ref, v_ref))
        scores = jnp.where(same, dot_t(q, k) * (SCALE * LOG2E), -1e30)
        top = jnp.max(scores, axis=-1, keepdims=True)
        weights = jnp.exp2(scores - top)
        total = jnp.sum(weights, axis=-1, keepdims=True)
        out = jnp.dot(weights.astype(jnp.bfloat16), v, preferred_element_type=jnp.float32) / total
        o_ref[:, :, cols] = out.astype(jnp.bfloat16).reshape(FRAMES, SPOTS, HEAD_DIM)


def temporal_attention(ct, qkv):
    block = (FRAMES, SPOTS, PER_STEP * HEAD_DIM)
    steps = ct // PER_STEP
    return pl.pallas_call(
        temporal_kernel,
        grid=(steps,),
        in_specs=[
            pl.BlockSpec(block, lambda h: (0, 0, h)),
            pl.BlockSpec(block, lambda h: (0, 0, steps + h)),
            pl.BlockSpec(block, lambda h: (0, 0, 2 * steps + h)),
        ],
        out_specs=pl.BlockSpec(block, lambda h: (0, 0, h)),
        out_shape=jax.ShapeDtypeStruct((FRAMES, SPOTS, ct * HEAD_DIM), jnp.bfloat16),
        compiler_params=pltpu.CompilerParams(vmem_limit_bytes=VMEM),
        cost_estimate=pl.CostEstimate(
            flops=ct * 256 * 256 * 128 * 4,
            bytes_accessed=ct * 2**18,
            transcendentals=ct * 256 * 256,
        ),
        name="temporal",
    )(qkv, qkv, qkv)


def exchange(x, group):
    return lax.all_to_all(x, group, split_axis=0, concat_axis=0, tiled=True)


def spot(z, c, yh):
    return z * 4 + c * 2 + yh


def send(x, pairs):
    return lax.ppermute(x, SPOT_GROUP, [(spot(*a), spot(*b)) for a, b in pairs])


def along_z(kv, halves):
    z = lax.axis_index("z")
    z1, z3, z2 = (send(kv, [((0, 0, h), (i, 0, h)) for h in halves]) for i in (1, 3, 2))
    return jnp.where(z == 0, kv, jnp.where(z == 1, z1, jnp.where(z == 2, z2, z3)))


def along_y(ring):
    across = send(ring, [((i, 0, 0), (i, 0, 1)) for i in range(4)])
    return jnp.where(lax.axis_index("yh") == 0, ring, across)


def to_core(ring):
    pairs = [((i, 0, h), (i, 1, h)) for i in range(4) for h in range(2)]
    return jnp.where(lax.axis_index("c") == 0, ring, send(ring, pairs))


def along(x, axis, step):
    return lax.ppermute(x, axis, [(i, (i + step) % 4) for i in range(4)])


Y_AXIS = ("yh", "yl")


def place_x():
    return lax.axis_index("x")


def place_y():
    return lax.axis_index("yh") * 2 + lax.axis_index("yl")


def run_copies(copies):
    for copy in copies:
        copy.start()
    for copy in copies:
        copy.wait()


def shuffle(kernel, outs, n_copies, name, *args):
    return pl.pallas_call(
        kernel,
        out_shape=tuple(jax.ShapeDtypeStruct(shape, jnp.bfloat16) for shape in outs),
        in_specs=[pl.BlockSpec(memory_space=pl.ANY)] * len(args),
        out_specs=(pl.BlockSpec(memory_space=pltpu.VMEM),) * len(outs),
        scratch_shapes=[pltpu.SemaphoreType.DMA((n_copies,))],
        compiler_params=pltpu.CompilerParams(vmem_limit_bytes=VMEM),
        name=name,
    )(*args)


def pick_kernel(ref, *refs):
    outs, sems = refs[:4], refs[4]
    y = place_y()
    run_copies(
        [
            pltpu.make_async_copy(ref.at[pl.ds((y + step) % 4 * 4, 4)], out, sems.at[step])
            for step, out in enumerate(outs)
        ]
    )


def turn_kernel(*refs):
    ins, outs, sems = refs[:4], refs[4:8], refs[8]
    x, y = place_x(), place_y()
    run_copies(
        [
            pltpu.make_async_copy(
                ref.at[(x + step) % 4], out.at[(y + 4 - back) % 4], sems.at[4 * step + back]
            )
            for step, out in enumerate(outs)
            for back, ref in enumerate(ins)
        ]
    )


def settle_kernel(*refs):
    ins, out, sems = refs[:4], refs[4], refs[5]
    x = place_x()
    run_copies(
        [
            pltpu.make_async_copy(
                ref.at[y], out.at[4 * y + (x + 4 - back) % 4], sems.at[4 * back + y]
            )
            for back, ref in enumerate(ins)
            for y in range(4)
        ]
    )


def attend(a, b, ct, queries, keys, values, head_kind):
    z, c, yh = (lax.axis_index(name) for name in SPOT_GROUP)
    arrays = (head_kind, queries, keys, values)
    wide, narrow = 2 * RANKS, RANKS
    spatial = HEADS - jnp.sum(head_kind)

    def unit(first, base, group, groups, width):
        held = (spatial - base - lax.axis_index(group) + groups - 1) // groups
        return jnp.stack([first.astype(jnp.int32), jnp.clip(held, 0, width)])

    if b:
        base = a * wide
        plan = [(0, part, b, base, narrow, name) for part, name in enumerate("qkv")]
        (qkv_send,) = pack(plan, [(narrow, ROWS, 3 * b * HEAD_DIM)], *arrays)
        qkv_b = exchange(qkv_send, FRAME_GROUP)

    plan = [(0, part, a, 0, wide, name) for part, name in enumerate("kv")]
    (kv_send,) = pack(plan, [(wide, ROWS, 2 * a * HEAD_DIM)], *arrays)
    plan = [(0, 0, a, 0, wide, "q")]
    plan += [(1, part, ct, None, 1, name) for part, name in enumerate("qkv")]
    shapes = [(wide, ROWS, a * HEAD_DIM), (1, ROWS, 3 * ct * HEAD_DIM)]
    q_send, t_send = pack(plan, shapes, *arrays)
    if b:
        qkv_b, kv_send, q_send, t_send = lax.optimization_barrier((qkv_b, kv_send, q_send, t_send))
    kv_a = exchange(kv_send, BLOCK_GROUP)
    if b:
        zero_b = to_core(along_y(along_z(qkv_b[:, :, b * HEAD_DIM :], (0,))))

    kv_a, q_send = lax.optimization_barrier((kv_a, q_send))
    q_a = exchange(q_send, BLOCK_GROUP)
    ring_a = along_z(kv_a[:RANKS], (0, 1))

    t_send = t_send.reshape(FRAMES, SPOTS, 3 * ct * HEAD_DIM)
    if b:
        q_a, ring_a, zero_b, t_send = lax.optimization_barrier((q_a, ring_a, zero_b, t_send))
    else:
        q_a, ring_a, t_send = lax.optimization_barrier((q_a, ring_a, t_send))
    t_have = exchange(t_send, SPOT_GROUP)

    at = unit(z + c == 0, 0, BLOCK_GROUP, wide, a)
    layouts = [(a, 0, wide)]
    if b:
        at_b = unit(z + c + yh == 0, a * wide, FRAME_GROUP, narrow, b)
        out_b = spatial_attention(b, 1, at_b, qkv_b, qkv_b, b, zero_b)
        q_a, out_b = lax.optimization_barrier((q_a, out_b))
        layouts.append((b, a * wide, narrow))
    out = spatial_attention(a, 2, at, q_a, kv_a, 0, to_core(ring_a))

    part = [(4, ROWS, a * HEAD_DIM)] * 4
    to_y = shuffle(pick_kernel, part, 4, "pick", out)
    on_y = [to_y[0]] + [along(to_y[step], Y_AXIS, step) for step in (1, 2, 3)]
    t_have = lax.optimization_barrier((t_have, to_y, out_b if b else to_y))[0]
    t_out = temporal_attention(ct, t_have)
    backs = []
    if b:
        out_b, _ = lax.optimization_barrier((out_b, t_have))
        back_b = exchange(out_b, FRAME_GROUP)
        t_out, back_b = lax.optimization_barrier((t_out, back_b))
        backs.append(back_b)
    on_y, t_out = lax.optimization_barrier((on_y, t_out))
    to_x = shuffle(turn_kernel, part, 16, "turn", *on_y)
    t_out, to_x = lax.optimization_barrier((t_out, to_x))
    on_x = [to_x[0]] + [along(to_x[step], "x", step) for step in (1, 2, 3)]
    backs = list(shuffle(settle_kernel, [(16, ROWS, a * HEAD_DIM)], 16, "settle", *on_x)) + backs
    t_back = exchange(t_out, SPOT_GROUP).reshape(ROWS, ct * HEAD_DIM)
    return unpack(layouts, ct, head_kind, backs, t_back)


def on_device(queries, keys, values, head_kind):
    temporal = jnp.sum(head_kind)
    spatial = HEADS - temporal
    index = jnp.int32(len(CASES) - 1)
    for i in reversed(range(len(CASES))):
        a, b, ct = CASES[i]
        room = 2 * RANKS * a + RANKS * b
        index = jnp.where(jnp.logical_and(spatial <= room, temporal <= ct), i, index)
    branches = [functools.partial(attend, *case) for case in CASES]
    return lax.switch(index, branches, queries, keys, values, head_kind)


def solution(mesh):
    fine = Mesh(mesh.devices.reshape(4, 2, 2, 2, 4), ("z", "c", "yh", "yl", "x"))
    rows = P(("z", "c", "yh", "yl", "x"), None)
    return jax.shard_map(
        on_device, mesh=fine, in_specs=(rows, rows, rows, P()), out_specs=rows, check_vma=False
    )
```
